256 devices in a mesh: tm: 16 (over x, y), space: 16 (over z, core).
Axes of the slice: x: 4, y: 4, z: 8, core: 2. Of those that a mesh axis runs over, the one named last changes fastest.
Arguments:
- snapshots: float32 [4096, 131072], P('tm', 'space'), may hold values from -300 to 300
- start: float32 [64, 2, 3, 32], replicated, may hold values from -6 to 6
Outputs:
- modes: float32 [64, 2, 3, 131072], P('tm', None, None, 'space')
- energies: float32 [64, 3], P('tm')
The draws below stay inside these ranges and needn't reach their ends.
All inputs are finite; a program needn't handle non-finite values.
Results may differ from the reference program's by a relative error of at most 0.0003.
Values sent between devices are 32-bit elements; how exact they have to be, the bound alone decides.
No kernel may reach another device: no remote copies, remote signals or barrier semaphores. Data moves between devices by JAX's collectives and lax.ppermute only.
A program may use at most 128 MiB of HBM per device.

```python
import math
import jax
import jax.numpy as jnp
from jax import lax

NFFT = 128
FREQS = 64
NB = 32
MODES = 3
ITERS = 2
NP = 131072
SNAPS = 4096


def draw_snapshots(key, part):
    key = jax.random.fold_in(key, 11)
    key_noise, key_time, key_pattern = jax.random.split(key, 3)
    strengths = (1.0, 0.75, 0.55, 0.4)
    position = jnp.arange(NP, dtype=jnp.float32) / NP
    noise_field = jax.random.truncated_normal(key_noise, -5.0, 5.0, (SNAPS, NP), jnp.float32)
    rise_factor = 3.0
    coherent_time = jax.random.truncated_normal(key_time, -4.0, 4.0, (SNAPS, 4), jnp.float32)
    patterns = jax.random.truncated_normal(key_pattern, -4.0, 4.0, (4, NP), jnp.float32)
    signal = noise_field
    for which in range(4):
        signal = signal + strengths[which] * coherent_time[:, which:which + 1] * patterns[which:which + 1, :]
    amplitude = jnp.exp(0.5 * math.log(rise_factor) * position)
    return signal * amplitude[None, :]


def noise(rng, shape, deviation, bound, kind=jnp.bfloat16):
    values = jax.random.normal(rng, shape, jnp.float32) * deviation
    return jnp.minimum(jnp.maximum(values, -bound), bound).astype(kind)


def setup_inputs(seed: int = 0) -> dict:
    arg_keys = jax.random.split(jax.random.key(seed), 3)
    snapshots = draw_snapshots(jax.random.fold_in(arg_keys[2], 71), 0)
    start = noise(arg_keys[1], (FREQS, 2, MODES, NB), 1.0, 6.0, jnp.float32)
    return {"snapshots": snapshots, "start": start}


EPSILON = 1e-06

def dft_table():
    time_ids = jnp.arange(NFFT, dtype=jnp.int32)
    freq_ids = jnp.arange(FREQS, dtype=jnp.int32)
    phase_ids = freq_ids[:, None] * time_ids[None, :] % NFFT
    angles = phase_ids.astype(jnp.float32) * (2.0 * math.pi / NFFT)
    window = 0.5 - 0.5 * jnp.cos(time_ids.astype(jnp.float32) * (2.0 * math.pi / NFFT))
    norm_scale = math.sqrt(8.0 / (3.0 * NFFT))
    cos_rows = jnp.cos(angles) * window[None, :] * norm_scale
    sin_rows = -jnp.sin(angles) * window[None, :] * norm_scale
    return jnp.stack([cos_rows, sin_rows], axis=1).reshape(2 * FREQS, NFFT)

def transform(block_data, basis_rows):
    block_count, _, point_count = block_data.shape
    product = jnp.einsum('kt,btx->kbx', basis_rows, block_data, precision=lax.Precision.HIGHEST)
    return product.reshape(FREQS, 2, block_count, point_count)

def partial_grams(spectra, total_points):
    freq_count, _, block_count, point_count = spectra.shape
    stacked = spectra.reshape(freq_count, 2 * block_count, point_count)
    products = jnp.einsum('fan,fcn->fac', stacked, stacked, precision=lax.Precision.HIGHEST) / (block_count * total_points)
    g_real = products[:, :block_count, :block_count] + products[:, block_count:, block_count:]
    g_imag = products[:, :block_count, block_count:] - products[:, block_count:, :block_count]
    return jnp.stack([g_real, g_imag], axis=1)

def batched(left, right):
    return jnp.einsum('fab,fmb->fma', left, right, precision=lax.Precision.HIGHEST)

def apply_gram(gram_parts, vectors):
    g_real, g_imag = (gram_parts[:, 0], gram_parts[:, 1])
    v_real, v_imag = (vectors[:, 0], vectors[:, 1])
    return jnp.stack([batched(g_real, v_real) - batched(g_imag, v_imag), batched(g_real, v_imag) + batched(g_imag, v_real)], axis=1)

def orthonormal(vectors):
    columns = []
    for which in range(vectors.shape[2]):
        column = vectors[:, :, which, :]
        for earlier in columns:
            proj_real = lax.optimization_barrier(jnp.sum(earlier[:, 0] * column[:, 0] + earlier[:, 1] * column[:, 1], axis=-1, keepdims=True))
            proj_imag = lax.optimization_barrier(jnp.sum(earlier[:, 0] * column[:, 1] - earlier[:, 1] * column[:, 0], axis=-1, keepdims=True))
            column = column - jnp.stack([earlier[:, 0] * proj_real - earlier[:, 1] * proj_imag, earlier[:, 0] * proj_imag + earlier[:, 1] * proj_real], axis=1)
        col_norm = jnp.sqrt(lax.optimization_barrier(jnp.sum(column * column, axis=(1, 2), keepdims=True)) + EPSILON)
        columns.append(column / col_norm)
    return jnp.stack(columns, axis=2)

def leading(gram_parts, start):
    vectors = orthonormal(start)
    for sweep in range(ITERS):
        vectors = orthonormal(apply_gram(gram_parts, vectors))
    rayleigh = lax.optimization_barrier(jnp.sum(vectors * apply_gram(gram_parts, vectors), axis=(1, 3)))
    weights = vectors / jnp.sqrt(vectors.shape[3] * rayleigh)[:, None, :, None]
    return (rayleigh, weights)

def reconstruct(spectra, weights):
    freq_count, _, block_count, point_count = spectra.shape
    mode_count = weights.shape[2]
    w_real, w_imag = (weights[:, 0], weights[:, 1])
    coeffs = jnp.stack([jnp.concatenate([w_real, -w_imag], axis=-1), jnp.concatenate([w_imag, w_real], axis=-1)], axis=1)
    coeffs = coeffs.reshape(freq_count, 2 * mode_count, 2 * block_count)
    stacked = spectra.reshape(freq_count, 2 * block_count, point_count)
    result = jnp.einsum('fkc,fcn->fkn', coeffs, stacked, precision=lax.Precision.HIGHEST)
    return result.reshape(freq_count, 2, mode_count, point_count)

def reference(snapshots, start):
    basis_rows = dft_table()
    spectra = transform(snapshots.reshape(NB, NFFT, NP), basis_rows)
    gram_parts = partial_grams(spectra, NP)
    energies, weights = leading(gram_parts, start)
    modes = reconstruct(spectra, weights)
    return (modes, energies)
```

```python
import functools
import math

import jax
import jax.numpy as jnp
import numpy as np
from jax import lax
from jax.experimental import pallas as pl
from jax.experimental.pallas import tpu as pltpu
from jax.sharding import PartitionSpec as P

NFFT = 128
FREQS = 64
NB = 32
MODES = 3
ITERS = 2
EPSILON = 1e-06
F32 = jnp.float32
BF16 = jnp.bfloat16
EXACT = lax.Precision.HIGHEST
VMEM_LIMIT = 48 * 1024 * 1024


def dft_table():
    time_ids = np.arange(NFFT)
    phase = np.arange(FREQS)[:, None] * time_ids[None, :] % NFFT
    angles = phase * (2.0 * math.pi / NFFT)
    window = 0.5 - 0.5 * np.cos(time_ids * (2.0 * math.pi / NFFT))
    scaled = window[None, :] * math.sqrt(8.0 / (3.0 * NFFT))
    return np.stack([np.cos(angles) * scaled, -np.sin(angles) * scaled], axis=1)


def send_rows(owners, local_blocks):
    table = dft_table().reshape(owners, 1, -1, NFFT)
    rows = np.zeros((owners, local_blocks, table.shape[2], local_blocks, NFFT))
    for block in range(local_blocks):
        rows[:, block, :, block, :] = table[:, 0]
    rows = rows.reshape(-1, local_blocks * NFFT).astype(np.float32)
    high = rows.astype(BF16)
    low = (rows - high.astype(np.float32)).astype(BF16)
    return high, low


def split(value):
    high = value.astype(BF16)
    return high, (value - high.astype(F32)).astype(BF16)


def dot(left, right):
    return jnp.dot(left, right, preferred_element_type=F32)


def exact_dot(left, right):
    return jnp.dot(left, right, precision=EXACT, preferred_element_type=F32)


def iota(shape, dim):
    return lax.broadcasted_iota(jnp.int32, shape, dim)


def transform_kernel(high_ref, low_ref, x_ref, out_ref):
    x_high, x_low = split(x_ref[...])
    high = high_ref[...]
    out = dot(high, x_high) + (dot(high, x_low) + dot(low_ref[...], x_high))
    out_ref[...] = out.reshape(out_ref.shape)


def transform(snapshots, owners):
    times, points = snapshots.shape
    local_blocks = times // NFFT
    high, low = send_rows(owners, local_blocks)
    tile = min(2048, points)
    per_owner = high.shape[0] // owners
    whole = pl.BlockSpec(high.shape, lambda i: (0, 0))
    return pl.pallas_call(
        transform_kernel,
        grid=(points // tile,),
        in_specs=[whole, whole, pl.BlockSpec((times, tile), lambda i: (0, i))],
        out_specs=pl.BlockSpec((owners, per_owner, tile), lambda i: (0, 0, i)),
        out_shape=jax.ShapeDtypeStruct((owners, per_owner, points), F32),
        compiler_params=pltpu.CompilerParams(vmem_limit_bytes=VMEM_LIMIT),
        name="transform",
    )(jnp.asarray(high), jnp.asarray(low), snapshots)


def gram_kernel(bins, scale, copies, s_ref, out_ref, same_ref, cross_ref):
    step = pl.program_id(0)
    rows = s_ref.shape[0] * s_ref.shape[1]
    half = rows // 2

    @pl.when(step == 0)
    def _():
        same_ref[...] = jnp.zeros_like(same_ref)
        cross_ref[...] = jnp.zeros_like(cross_ref)

    high, low = split(s_ref[...].reshape(rows, s_ref.shape[2]))
    contract = (((1,), (1,)), ((), ()))
    same_ref[...] += lax.dot_general(high, high, contract, preferred_element_type=F32)
    cross_ref[...] += lax.dot_general(high, low, contract, preferred_element_type=F32)

    @pl.when(step == pl.num_programs(0) - 1)
    def _():
        cross = cross_ref[...]
        full = (same_ref[...] + (cross + cross.T)) * scale
        row, col = iota((rows, rows), 0), iota((rows, rows), 1)
        full = jnp.where((row >> 1) % bins == (col >> 1) % bins, full, 0.0)
        spread = jnp.where(col == (row & 1) * half + (row >> 1), 1.0, 0.0)
        row, col = iota((2 * NB, rows), 0), iota((2 * NB, rows), 1)
        fold = jnp.where(row == (col & 1) * NB + (col >> 1) // bins, 1.0, 0.0)
        part = exact_dot(exact_dot(fold, full), spread)
        real = part[:NB, :half] + part[NB:, half:]
        imag = part[NB:, :half] - part[:NB, half:]
        both = jnp.concatenate([real, imag], axis=1)
        for copy in range(copies):
            out_ref[copy] = both


def partial_gram(spectra, bins, total_points, copies):
    owners, per_owner, points = spectra.shape
    rows = owners * per_owner
    tile = min(2048, points)
    scale = 1.0 / (NB * total_points)
    return pl.pallas_call(
        functools.partial(gram_kernel, bins, scale, copies),
        grid=(points // tile,),
        in_specs=[pl.BlockSpec((owners, per_owner, tile), lambda i: (0, 0, i))],
        out_specs=pl.BlockSpec((copies, NB, rows), lambda i: (0, 0, 0)),
        out_shape=jax.ShapeDtypeStruct((copies, NB, rows), F32),
        scratch_shapes=[pltpu.VMEM((rows, rows), F32), pltpu.VMEM((rows, rows), F32)],
        compiler_params=pltpu.CompilerParams(vmem_limit_bytes=VMEM_LIMIT),
        name="gram",
    )(spectra)


def block_sum(value, bins):
    shift = bins
    while shift < value.shape[1]:
        value = value + pltpu.roll(value, shift, 1)
        shift *= 2
    return value


def orthonormal(real, imag, bins):
    done = []
    for which in range(MODES):
        c_real, c_imag = real[which : which + 1], imag[which : which + 1]
        for e_real, e_imag in done:
            proj_real = block_sum(e_real * c_real + e_imag * c_imag, bins)
            proj_imag = block_sum(e_real * c_imag - e_imag * c_real, bins)
            c_real, c_imag = (
                c_real - (e_real * proj_real - e_imag * proj_imag),
                c_imag - (e_real * proj_imag + e_imag * proj_real),
            )
        norm = jnp.sqrt(block_sum(c_real * c_real + c_imag * c_imag, bins) + EPSILON)
        done.append((c_real / norm, c_imag / norm))
    pad = [jnp.zeros((8 - MODES, real.shape[1]), F32)]
    return (
        jnp.concatenate([c[0] for c in done] + pad, axis=0),
        jnp.concatenate([c[1] for c in done] + pad, axis=0),
    )


def apply_gram(gram, real, imag):
    lanes = real.shape[1]
    product = exact_dot(jnp.concatenate([real, imag], axis=0), gram)
    return (
        product[:8, :lanes] - product[8:, lanes:],
        product[8:, :lanes] + product[:8, lanes:],
    )


def leading(gram_parts, start, bins):
    lanes = start.shape[1]
    total = gram_parts[0]
    for part in gram_parts[1:]:
        total = total + part
    row, col = iota((lanes, NB), 0), iota((lanes, NB), 1)
    spread = jnp.where(row // bins == col, 1.0, 0.0)
    gram = exact_dot(spread, total)
    row, col = iota(gram.shape, 0), iota(gram.shape, 1)
    gram = jnp.where(row % bins == col % bins, gram, 0.0)
    real, imag = orthonormal(start[:8], start[8:], bins)
    for _ in range(ITERS):
        real, imag = orthonormal(*apply_gram(gram, real, imag), bins)
    g_real, g_imag = apply_gram(gram, real, imag)
    rayleigh = block_sum(real * g_real + imag * g_imag, bins)
    norm = jnp.sqrt(NB * rayleigh)
    used = iota(real.shape, 0) < MODES
    return (
        jnp.where(used, real / norm, 0.0),
        jnp.where(used, imag / norm, 0.0),
        rayleigh,
    )


def modes_kernel(bins, gram_ref, start_ref, s_ref, modes_ref, energy_ref, coef_ref):
    rows = s_ref.shape[0] * s_ref.shape[1]
    half = rows // 2

    @pl.when(pl.program_id(0) == 0)
    def _():
        parts = [gram_ref[i] for i in range(gram_ref.shape[0])]
        real, imag, rayleigh = leading(parts, start_ref[...], bins)
        energy_ref[...] = rayleigh
        row, col = iota((half, rows), 0), iota((half, rows), 1)
        to_real = jnp.where(col == 2 * row, 1.0, 0.0)
        to_imag = jnp.where(col == 2 * row + 1, 1.0, 0.0)
        coefs = (
            exact_dot(real, to_real) - exact_dot(imag, to_imag),
            exact_dot(imag, to_real) + exact_dot(real, to_imag),
        )
        owner = (iota((8, rows), 1) >> 1) % bins
        stacked = jnp.concatenate(
            [jnp.where(owner == k, coefs[p], 0.0) for k in range(bins) for p in range(2)],
            axis=0,
        )
        high, low = split(stacked)
        coef_ref[0] = high
        coef_ref[1] = low

    s_high, s_low = split(s_ref[...].reshape(rows, s_ref.shape[2]))
    c_high, c_low = coef_ref[0], coef_ref[1]
    out = dot(c_high, s_high) + (dot(c_high, s_low) + dot(c_low, s_high))
    for k in range(bins):
        for p in range(2):
            at = (2 * k + p) * 8
            modes_ref[k, p] = out[at : at + MODES]


def modes_of(gram_parts, start, spectra, bins):
    owners, per_owner, points = spectra.shape
    rows = owners * per_owner
    tile = min(2048, points)
    lanes = start.shape[1]
    return pl.pallas_call(
        functools.partial(modes_kernel, bins),
        grid=(points // tile,),
        in_specs=[
            pl.BlockSpec(gram_parts.shape, lambda i: (0, 0, 0)),
            pl.BlockSpec(start.shape, lambda i: (0, 0)),
            pl.BlockSpec((owners, per_owner, tile), lambda i: (0, 0, i)),
        ],
        out_specs=[
            pl.BlockSpec((bins, 2, MODES, tile), lambda i: (0, 0, 0, i)),
            pl.BlockSpec((8, lanes), lambda i: (0, 0)),
        ],
        out_shape=[
            jax.ShapeDtypeStruct((bins, 2, MODES, points), F32),
            jax.ShapeDtypeStruct((8, lanes), F32),
        ],
        scratch_shapes=[pltpu.VMEM((2, 16 * bins, rows), BF16)],
        compiler_params=pltpu.CompilerParams(vmem_limit_bytes=VMEM_LIMIT),
        name="modes",
    )(gram_parts, start, spectra)


def on_device(snapshots, start):
    tm_count = lax.axis_size("tm")
    space_count = lax.axis_size("space")
    total_points = snapshots.shape[1] * space_count
    bins = FREQS // tm_count
    first = lax.axis_index("tm") * bins
    own = lax.dynamic_slice_in_dim(start, first, bins, 0)
    own = jnp.pad(own.transpose(1, 2, 3, 0), ((0, 0), (0, 8 - MODES), (0, 0), (0, 0)))
    own = own.reshape(16, NB * bins)
    sent = transform(snapshots, tm_count)
    spectra = lax.all_to_all(sent, "tm", split_axis=0, concat_axis=0, tiled=True)
    gram = partial_gram(spectra, bins, total_points, space_count)
    grams = lax.all_to_all(gram, "space", split_axis=0, concat_axis=0, tiled=True)
    modes, rayleigh = modes_of(grams, own, spectra, bins)
    return (modes, rayleigh[:MODES, :bins].T)


def solution(mesh):
    in_specs = (P("tm", "space"), P())
    out_specs = (P("tm", None, None, "space"), P("tm", None))
    return jax.shard_map(
        on_device, mesh=mesh, in_specs=in_specs, out_specs=out_specs, check_vma=False
    )
```

```python
import functools
import math

import jax
import jax.numpy as jnp
import numpy as np
from jax import lax
from jax.experimental import pallas as pl
from jax.experimental.pallas import tpu as pltpu
from jax.sharding import PartitionSpec as P

NFFT = 128
FREQS = 64
NB = 32
MODES = 3
ITERS = 2
EPSILON = 1e-06
F32 = jnp.float32
BF16 = jnp.bfloat16
CHUNK = 2048
VMEM_LIMIT = 24 * 1024 * 1024
HBM = pl.BlockSpec(memory_space=pltpu.HBM)
VMEM = pl.BlockSpec(memory_space=pltpu.VMEM)


def dft_table():
    time_ids = np.arange(NFFT)
    phase = np.arange(FREQS)[:, None] * time_ids[None, :] % NFFT
    angles = phase * (2.0 * math.pi / NFFT)
    window = 0.5 - 0.5 * np.cos(time_ids * (2.0 * math.pi / NFFT))
    scaled = window[None, :] * math.sqrt(8.0 / (3.0 * NFFT))
    table = np.stack([np.cos(angles) * scaled, -np.sin(angles) * scaled], axis=1)
    return table.reshape(2 * FREQS, NFFT).astype(np.float32)


def split(value):
    high = value.astype(BF16)
    return high, (value - high.astype(F32)).astype(BF16)


def split3(value):
    high = value.astype(BF16)
    rest = value - high.astype(F32)
    middle = rest.astype(BF16)
    return high, middle, (rest - middle.astype(F32)).astype(BF16)


def dot(left, right):
    return jnp.dot(left, right, preferred_element_type=F32)


def dot_rows(left, right):
    return lax.dot_general(left, right, (((1,), (1,)), ((), ())), preferred_element_type=F32)


def pick_right(value, select):
    high, middle, low = split3(value)
    return dot(high, select) + (dot(middle, select) + dot(low, select))


def pick_left(select, value):
    high, middle, low = split3(value)
    return dot(select, high) + (dot(select, middle) + dot(select, low))


def iota(shape, dim):
    return lax.broadcasted_iota(jnp.int32, shape, dim)


def ones_where(condition):
    return jnp.where(condition, 1.0, 0.0).astype(BF16)


def column_chunks(points):
    size = min(CHUNK, points)
    return [(at, size) for at in range(0, points, size)]


def first_vectors(start, first, bins):
    lanes = NB * bins
    rows, freqs = 2 * MODES * NB, start.shape[3]
    row, col = iota((freqs, lanes), 0), iota((freqs, lanes), 1)
    picked = pick_right(start.reshape(rows, freqs), ones_where(row == first + col % bins))
    picked = jnp.where(iota((rows, lanes), 0) % NB == iota((rows, lanes), 1) // bins, picked, 0.0)
    picked = jnp.sum(picked.reshape(2 * MODES, NB, lanes), axis=1)
    vectors = [(picked[m : m + 1], picked[MODES + m : MODES + m + 1]) for m in range(MODES)]
    vectors = orthonormal(vectors, bin_ones(lanes, bins))
    return jnp.concatenate([stack8(vectors, 0), stack8(vectors, 1)], axis=0)


def transform_kernel(
    owners, table_hbm, x_hbm, start_hbm, out_ref, first_ref, table_ref, x_ref, start_ref, in_sem, small_sem
):
    times, points = x_hbm.shape
    local_blocks = times // NFFT
    chunks = column_chunks(points)

    def fetch(i):
        at, size = chunks[i]
        cols = pl.ds(at, size)
        return pltpu.make_async_copy(x_hbm.at[:, cols], x_ref.at[:, cols], in_sem.at[i])

    table_copy = pltpu.make_async_copy(table_hbm, table_ref, small_sem.at[0])
    start_copy = pltpu.make_async_copy(start_hbm, start_ref, small_sem.at[1])
    table_copy.start()
    start_copy.start()
    for i in range(len(chunks)):
        fetch(i).start()
    bins = FREQS // owners
    start_copy.wait()
    first_ref[...] = first_vectors(start_ref[...], lax.axis_index("tm") * bins, bins)
    table_copy.wait()
    table = table_ref[...].reshape(owners, -1, NFFT)
    blank = jnp.zeros_like(table)
    rows = [
        jnp.concatenate([table if c == b else blank for c in range(local_blocks)], axis=2)
        for b in range(local_blocks)
    ]
    rows = jnp.concatenate(rows, axis=1).reshape(-1, times)
    high, low = split(rows)
    for i, (at, size) in enumerate(chunks):
        fetch(i).wait()
        x_high, x_low = split(x_ref[:, at : at + size])
        out = dot(high, x_high) + (dot(high, x_low) + dot(low, x_high))
        out_ref[:, :, at : at + size] = out.reshape(owners, -1, size)


def transform(snapshots, start, owners):
    times, points = snapshots.shape
    shape = (owners, 2 * FREQS // owners * (times // NFFT), points)
    count = len(column_chunks(points))
    table = pltpu.with_memory_space_constraint(jnp.asarray(dft_table()), pltpu.HBM)
    return pl.pallas_call(
        functools.partial(transform_kernel, owners),
        in_specs=[HBM, HBM, HBM],
        out_specs=[VMEM, VMEM],
        out_shape=[
            pltpu.VMEM(shape, F32),
            jax.ShapeDtypeStruct((16, NB * FREQS // owners), F32),
        ],
        scratch_shapes=[
            pltpu.VMEM((2 * FREQS, NFFT), F32),
            pltpu.VMEM(snapshots.shape, F32),
            pltpu.VMEM(start.shape, F32),
            pltpu.SemaphoreType.DMA((count,)),
            pltpu.SemaphoreType.DMA((2,)),
        ],
        compiler_params=pltpu.CompilerParams(vmem_limit_bytes=24 * 1024 * 1024),
        name="transform",
    )(table, snapshots, start)


def gram_kernel(bins, scale, s_ref, out_ref):
    rows = s_ref.shape[0] * s_ref.shape[1]
    half = rows // 2
    row, col = iota((rows, rows), 0), iota((rows, rows), 1)
    same_bin = (row >> 1) % bins == (col >> 1) % bins
    spread = ones_where(col == (row & 1) * half + (row >> 1))
    row, col = iota((2 * NB, rows), 0), iota((2 * NB, rows), 1)
    fold = ones_where(row == (col & 1) * NB + (col >> 1) // bins)
    same = jnp.zeros((rows, rows), F32)
    cross = jnp.zeros((rows, rows), F32)
    for at, size in column_chunks(s_ref.shape[2]):
        high, low = split(s_ref[:, :, at : at + size].reshape(rows, size))
        same += dot_rows(high, high)
        cross += dot_rows(high, low)
    full = (same + (cross + cross.T)) * scale
    full = jnp.where(same_bin, full, 0.0)
    part = pick_right(pick_left(fold, full), spread)
    real = part[:NB, :half] + part[NB:, half:]
    imag = part[NB:, :half] - part[:NB, half:]
    packed = jnp.where(iota(real.shape, 0) <= iota(real.shape, 1) // bins, real, imag)
    for copy in range(out_ref.shape[0]):
        out_ref[copy] = packed


def partial_gram(spectra, bins, total_points, copies):
    owners, per_owner, points = spectra.shape
    lanes = owners * per_owner // 2
    return pl.pallas_call(
        functools.partial(gram_kernel, bins, 1.0 / (NB * total_points)),
        in_specs=[VMEM],
        out_specs=VMEM,
        out_shape=pltpu.VMEM((copies, NB, lanes), F32),
        compiler_params=pltpu.CompilerParams(vmem_limit_bytes=VMEM_LIMIT),
        name="gram",
    )(spectra)


def bin_ones(lanes, bins):
    return ones_where(iota((lanes, lanes), 0) % bins == iota((lanes, lanes), 1) % bins)


def block_sums(terms, ones):
    stacked = jnp.concatenate(terms + [jnp.zeros((8 - len(terms), ones.shape[0]), F32)], axis=0)
    high, middle, low = split3(stacked)
    sums = dot(high, ones) + (dot(middle, ones) + dot(low, ones))
    return [sums[i : i + 1] for i in range(len(terms))]


def overlap(e, c):
    return [e[0] * c[0] + e[1] * c[1], e[0] * c[1] - e[1] * c[0]]


def orthonormal(vectors, ones):
    left = list(vectors)
    done = []
    while left:
        head = left.pop(0)
        terms = overlap(head, head)[:1]
        for other in left:
            terms = terms + overlap(head, other)
        sums = block_sums(terms, ones)
        norm = jnp.sqrt(sums[0] + EPSILON)
        unit = (head[0] / norm, head[1] / norm)
        for i in range(len(left)):
            real, imag = sums[1 + 2 * i] / norm, sums[2 + 2 * i] / norm
            left[i] = (
                left[i][0] - (unit[0] * real - unit[1] * imag),
                left[i][1] - (unit[0] * imag + unit[1] * real),
            )
        done.append(unit)
    return done


def stack8(vectors, part):
    blank = jnp.zeros((8 - len(vectors), vectors[0][0].shape[1]), F32)
    return jnp.concatenate([v[part] for v in vectors] + [blank], axis=0)


def apply_gram(gram, vectors):
    lanes = vectors[0][0].shape[1]
    both = jnp.concatenate([stack8(vectors, 0), stack8(vectors, 1)], axis=0)
    high, middle, low = split3(both)
    product = dot(high, gram[0]) + (
        (dot(high, gram[1]) + dot(middle, gram[0]))
        + (dot(middle, gram[1]) + (dot(high, gram[2]) + dot(low, gram[0])))
    )
    real = product[:8, :lanes] - product[8:, lanes:]
    imag = product[8:, :lanes] + product[:8, lanes:]
    return [(real[m : m + 1], imag[m : m + 1]) for m in range(MODES)]


def leading(total, start, bins):
    lanes = start.shape[1]
    ones = bin_ones(lanes, bins)
    vectors = [(start[m : m + 1], start[8 + m : 9 + m]) for m in range(MODES)]
    row, col = iota((lanes, NB), 0), iota((lanes, NB), 1)
    packed = pick_left(ones_where(row // bins == col), total)
    row, col = iota(packed.shape, 0), iota(packed.shape, 1)
    packed = jnp.where(row % bins == col % bins, packed, 0.0)
    turned = packed.T
    row, col = row // bins, col // bins
    real = jnp.where(row <= col, packed, turned)
    imag = jnp.where(row > col, packed, jnp.where(row < col, -turned, 0.0))
    gram = split3(jnp.concatenate([real, imag], axis=1))
    for _ in range(ITERS):
        vectors = orthonormal(apply_gram(gram, vectors), ones)
    images = apply_gram(gram, vectors)
    terms = [overlap(v, g)[0] for v, g in zip(vectors, images, strict=True)]
    energies = block_sums(terms, ones)
    weights = [
        (v[0] / jnp.sqrt(NB * e), v[1] / jnp.sqrt(NB * e))
        for v, e in zip(vectors, energies, strict=True)
    ]
    return stack8(weights, 0), stack8(weights, 1), energies


def modes_kernel(bins, grams_ref, start_ref, s_ref, modes_ref, energy_ref):
    rows = s_ref.shape[0] * s_ref.shape[1]
    half = rows // 2
    total = grams_ref[0]
    for i in range(1, grams_ref.shape[0]):
        total = total + grams_ref[i]
    real, imag, energies = leading(total, start_ref[...], bins)
    row, col = iota((half, 2 * rows), 0), iota((half, 2 * rows), 1)
    spread = ones_where(col == 2 * row + jnp.where(col < rows, 0, rows + 1))
    wide = pick_right(jnp.concatenate([real, imag], axis=0), spread)
    to_real = wide[:8, :rows] - wide[8:, rows:]
    to_imag = wide[8:, :rows] + wide[:8, rows:]
    owner = (iota((1, rows), 1) >> 1) % bins
    blank = jnp.zeros((6, rows), F32)
    groups = []
    for k in range(bins):
        for m in range(MODES):
            pair = jnp.concatenate([to_real[m : m + 1], to_imag[m : m + 1]], axis=0)
            groups += [jnp.where(owner == k, pair, 0.0), blank]
    c_both = jnp.concatenate(split(jnp.concatenate(groups, axis=0)), axis=0)
    used = c_both.shape[0] // 2
    for at, size in column_chunks(s_ref.shape[2]):
        s_high, s_low = split(s_ref[:, :, at : at + size].reshape(rows, size))
        both = dot(c_both, s_high)
        out = both[:used] + (both[used:] + dot(c_both[:used], s_low))
        for k in range(bins):
            for m in range(MODES):
                group = (k * MODES + m) * 8
                modes_ref[k, m, :, at : at + size] = out[group : group + 2]
    stacked = jnp.concatenate(energies + [jnp.zeros((8 - MODES, half), F32)], axis=0)
    energy_ref[...] = stacked.T[:bins, :MODES]


def modes_of(grams, start, spectra, bins):
    points = spectra.shape[2]
    return pl.pallas_call(
        functools.partial(modes_kernel, bins),
        in_specs=[VMEM, VMEM, VMEM],
        out_specs=[VMEM, VMEM],
        out_shape=[
            jax.ShapeDtypeStruct((bins, MODES, 2, points), F32),
            jax.ShapeDtypeStruct((bins, MODES), F32),
        ],
        compiler_params=pltpu.CompilerParams(vmem_limit_bytes=VMEM_LIMIT),
        name="modes",
    )(grams, start, spectra)


def on_device(snapshots, start):
    tm_count = lax.axis_size("tm")
    space_count = lax.axis_size("space")
    total_points = snapshots.shape[1] * space_count
    bins = FREQS // tm_count
    snapshots = pltpu.with_memory_space_constraint(snapshots, pltpu.HBM)
    start = pltpu.with_memory_space_constraint(start.transpose(1, 2, 3, 0), pltpu.HBM)
    sent, own = transform(snapshots, start, tm_count)
    spectra = lax.all_to_all(sent, "tm", split_axis=0, concat_axis=0, tiled=True)
    spectra = pltpu.with_memory_space_constraint(spectra, pltpu.VMEM)
    gram = partial_gram(spectra, bins, total_points, space_count)
    grams = lax.all_to_all(gram, "space", split_axis=0, concat_axis=0, tiled=True)
    modes, energies = modes_of(grams, own, spectra, bins)
    return (modes.transpose(0, 2, 1, 3), energies)


def solution(mesh):
    in_specs = (P("tm", "space"), P())
    out_specs = (P("tm", None, None, "space"), P("tm", None))
    return jax.shard_map(
        on_device, mesh=mesh, in_specs=in_specs, out_specs=out_specs, check_vma=False
    )
```

```python
import functools
import math

import jax
import jax.numpy as jnp
import numpy as np
from jax import lax
from jax.experimental import pallas as pl
from jax.experimental.pallas import tpu as pltpu
from jax.sharding import PartitionSpec as P

NFFT = 128
FREQS = 64
NB = 32
MODES = 3
ITERS = 2
EPSILON = 1e-06
BINS = 4
BLOCKS = 2
F32 = jnp.float32
BF16 = jnp.bfloat16
CHUNK = 2048
VMEM_LIMIT = 24 * 1024 * 1024
HBM = pl.BlockSpec(memory_space=pltpu.HBM)
VMEM = pl.BlockSpec(memory_space=pltpu.VMEM)


def dft_table():
    time_ids = np.arange(NFFT)
    phase = np.arange(FREQS)[:, None] * time_ids[None, :] % NFFT
    angles = phase * (2.0 * math.pi / NFFT)
    window = 0.5 - 0.5 * np.cos(time_ids * (2.0 * math.pi / NFFT))
    scaled = window[None, :] * math.sqrt(8.0 / (3.0 * NFFT))
    table = np.stack([np.cos(angles) * scaled, -np.sin(angles) * scaled], axis=1)
    return table.reshape(2 * FREQS, NFFT).astype(np.float32)


def split(value):
    high = value.astype(BF16)
    return high, (value - high.astype(F32)).astype(BF16)


def split3(value):
    high = value.astype(BF16)
    rest = value - high.astype(F32)
    middle = rest.astype(BF16)
    return high, middle, (rest - middle.astype(F32)).astype(BF16)


def dot(left, right):
    return jnp.dot(left, right, preferred_element_type=F32)


def dot_rows(left, right):
    return lax.dot_general(left, right, (((1,), (1,)), ((), ())), preferred_element_type=F32)


def pick_right(value, select):
    high, middle, low = split3(value)
    return dot(high, select) + (dot(middle, select) + dot(low, select))


def pick_left(select, value):
    high, middle, low = split3(value)
    return dot(select, high) + (dot(select, middle) + dot(select, low))


def iota(shape, dim):
    return lax.broadcasted_iota(jnp.int32, shape, dim)


def ones_where(condition):
    return jnp.where(condition, 1.0, 0.0).astype(BF16)


def row_order(row):
    pair = (row >> 3) & 1
    return (row >> 4) * BLOCKS + (((row >> 2) & 1) ^ pair), pair * 2 + ((row >> 1) & 1), row & 1


def column_chunks(points):
    size = min(CHUNK, points)
    return [(at, size) for at in range(0, points, size)]


def arrival_chunks(points):
    first = points // 4
    second = (points - first) // 2
    return [(0, first), (first, second), (first + second, points - first - second)]


def first_vectors(start, first, bins):
    lanes = NB * bins
    rows, freqs = 2 * MODES * NB, start.shape[3]
    row, col = iota((freqs, lanes), 0), iota((freqs, lanes), 1)
    picked = pick_right(start.reshape(rows, freqs), ones_where(row == first + col % bins))
    picked = jnp.where(iota((rows, lanes), 0) % NB == iota((rows, lanes), 1) // bins, picked, 0.0)
    picked = jnp.sum(picked.reshape(2 * MODES, NB, lanes), axis=1)
    vectors = [(picked[m : m + 1], picked[MODES + m : MODES + m + 1]) for m in range(MODES)]
    vectors = orthonormal(vectors, bin_ones(lanes, bins))
    return jnp.concatenate([stack8(vectors, 0), stack8(vectors, 1)], axis=0)


def transform_kernel(
    owners, table_hbm, x_hbm, start_hbm, out_ref, first_ref, table_ref, x_ref, start_ref, in_sem, small_sem
):
    times, points = x_hbm.shape
    local_blocks = times // NFFT
    chunks = arrival_chunks(points)

    def fetch(i):
        at, size = chunks[i]
        cols = pl.ds(at, size)
        return pltpu.make_async_copy(x_hbm.at[:, cols], x_ref.at[:, cols], in_sem.at[i])

    table_copy = pltpu.make_async_copy(table_hbm, table_ref, small_sem.at[0])
    start_copy = pltpu.make_async_copy(start_hbm, start_ref, small_sem.at[1])
    table_copy.start()
    start_copy.start()
    for i in range(len(chunks)):
        fetch(i).start()
    bins = FREQS // owners
    table_copy.wait()
    table = table_ref[...].reshape(owners, 2, -1, NFFT)
    table = [table, jnp.concatenate([table[:, 1:], table[:, :1]], axis=1)]
    table = [split(rows.reshape(-1, NFFT)) for rows in table]
    wide = [jnp.concatenate([high, low], axis=1) for high, low in table]
    for i, (at, size) in enumerate(chunks):
        fetch(i).wait()
        found = []
        for block in range(BLOCKS):
            x_high, x_low = split(x_ref[block * NFFT : (block + 1) * NFFT, at : at + size])
            twice = jnp.concatenate([x_high, x_high], axis=0)
            out = dot(wide[block], twice) + dot(table[block][0], x_low)
            found.append(out.reshape(owners, 8, size))
        upper = iota((owners, 8, size), 1) < 4
        out_ref[:, :8, at : at + size] = jnp.where(upper, found[0], found[1])
        out_ref[:, 8:, at : at + size] = jnp.where(upper, found[1], found[0])
        if i == 1:
            start_copy.wait()
            first = lax.axis_index("tm") * bins
            first_ref[...] = first_vectors(start_ref[...], first, bins)


def transform(snapshots, start, owners):
    times, points = snapshots.shape
    shape = (owners, 2 * FREQS // owners * (times // NFFT), points)
    count = len(arrival_chunks(points))
    table = pltpu.with_memory_space_constraint(jnp.asarray(dft_table()), pltpu.HBM)
    return pl.pallas_call(
        functools.partial(transform_kernel, owners),
        in_specs=[HBM, HBM, HBM],
        out_specs=[VMEM, VMEM],
        out_shape=[
            pltpu.VMEM(shape, F32),
            jax.ShapeDtypeStruct((16, NB * FREQS // owners), F32),
        ],
        scratch_shapes=[
            pltpu.VMEM((2 * FREQS, NFFT), F32),
            pltpu.VMEM(snapshots.shape, F32),
            pltpu.VMEM(start.shape, F32),
            pltpu.SemaphoreType.DMA((count,)),
            pltpu.SemaphoreType.DMA((2,)),
        ],
        compiler_params=pltpu.CompilerParams(vmem_limit_bytes=24 * 1024 * 1024),
        name="transform",
    )(table, snapshots, start)


def gram_kernel(scale, s_ref, out_ref):
    owners, _, points = s_ref.shape
    rows, half = owners * 8, NB * BINS
    sums = [jnp.zeros((2 * rows, rows), F32) for pair in range(2)]
    for at, size in column_chunks(points):
        for pair in range(2):
            value = s_ref[:, pair * 8 : pair * 8 + 8, at : at + size].reshape(rows, size)
            high, low = split(value)
            sums[pair] += dot_rows(jnp.concatenate([high, low], axis=0), high)
    part = jnp.zeros((2 * NB, 2 * half), F32)
    for pair in range(2):
        same, cross = sums[pair][:rows], sums[pair][rows:]
        full = (same + (cross + cross.T)) * scale
        row, col = iota((rows, rows), 0), iota((rows, rows), 1)
        full = jnp.where((row >> 1) & 1 == (col >> 1) & 1, full, 0.0)
        row, col = iota((2 * NB, rows), 0), iota((2 * NB, rows), 1)
        block, _, which = row_order((col >> 3) * 16 + pair * 8 + (col & 7))
        fold = ones_where(row == which * NB + block)
        row, col = iota((rows, 2 * half), 0), iota((rows, 2 * half), 1)
        block, own_bin, which = row_order((row >> 3) * 16 + pair * 8 + (row & 7))
        spread = ones_where(col == which * half + block * BINS + own_bin)
        part += pick_right(pick_left(fold, full), spread)
    real = part[:NB, :half] + part[NB:, half:]
    imag = part[NB:, :half] - part[:NB, half:]
    packed = jnp.where(iota(real.shape, 0) <= iota(real.shape, 1) // BINS, real, imag)
    out_ref[...] = packed


def partial_gram(spectra, total_points):
    return pl.pallas_call(
        functools.partial(gram_kernel, 1.0 / (NB * total_points)),
        in_specs=[VMEM],
        out_specs=VMEM,
        out_shape=pltpu.VMEM((NB, NB * BINS), F32),
        compiler_params=pltpu.CompilerParams(vmem_limit_bytes=VMEM_LIMIT),
        name="gram",
    )(spectra)


def bin_ones(lanes, bins):
    return ones_where(iota((lanes, lanes), 0) % bins == iota((lanes, lanes), 1) % bins)


def block_sums(terms, ones):
    stacked = jnp.concatenate(terms + [jnp.zeros((8 - len(terms), ones.shape[0]), F32)], axis=0)
    high, middle, low = split3(stacked)
    sums = dot(high, ones) + (dot(middle, ones) + dot(low, ones))
    return [sums[i : i + 1] for i in range(len(terms))]


def overlap(e, c):
    return [e[0] * c[0] + e[1] * c[1], e[0] * c[1] - e[1] * c[0]]


def orthonormal(vectors, ones):
    left = list(vectors)
    done = []
    while left:
        head = left.pop(0)
        terms = overlap(head, head)[:1]
        for other in left:
            terms = terms + overlap(head, other)
        sums = block_sums(terms, ones)
        norm = jnp.sqrt(sums[0] + EPSILON)
        unit = (head[0] / norm, head[1] / norm)
        for i in range(len(left)):
            real, imag = sums[1 + 2 * i] / norm, sums[2 + 2 * i] / norm
            left[i] = (
                left[i][0] - (unit[0] * real - unit[1] * imag),
                left[i][1] - (unit[0] * imag + unit[1] * real),
            )
        done.append(unit)
    return done


def stack8(vectors, part):
    blank = jnp.zeros((8 - len(vectors), vectors[0][0].shape[1]), F32)
    return jnp.concatenate([v[part] for v in vectors] + [blank], axis=0)


def apply_gram(gram, vectors):
    lanes = vectors[0][0].shape[1]
    both = jnp.concatenate([stack8(vectors, 0), stack8(vectors, 1)], axis=0)
    high, middle, low = split3(both)
    product = dot(high, gram[0]) + (
        (dot(high, gram[1]) + dot(middle, gram[0]))
        + (dot(middle, gram[1]) + (dot(high, gram[2]) + dot(low, gram[0])))
    )
    real = product[:8, :lanes] - product[8:, lanes:]
    imag = product[8:, :lanes] + product[:8, lanes:]
    return [(real[m : m + 1], imag[m : m + 1]) for m in range(MODES)]


def leading(total, start, bins):
    lanes = start.shape[1]
    ones = bin_ones(lanes, bins)
    vectors = [(start[m : m + 1], start[8 + m : 9 + m]) for m in range(MODES)]
    row, col = iota((lanes, NB), 0), iota((lanes, NB), 1)
    packed = pick_left(ones_where(row // bins == col), total)
    row, col = iota(packed.shape, 0), iota(packed.shape, 1)
    packed = jnp.where(row % bins == col % bins, packed, 0.0)
    turned = packed.T
    row, col = row // bins, col // bins
    real = jnp.where(row <= col, packed, turned)
    imag = jnp.where(row > col, packed, jnp.where(row < col, -turned, 0.0))
    gram = split3(jnp.concatenate([real, imag], axis=1))
    for _ in range(ITERS):
        vectors = orthonormal(apply_gram(gram, vectors), ones)
    images = apply_gram(gram, vectors)
    terms = [overlap(v, g)[0] for v, g in zip(vectors, images, strict=True)]
    energies = block_sums(terms, ones)
    weights = [
        (v[0] / jnp.sqrt(NB * e), v[1] / jnp.sqrt(NB * e))
        for v, e in zip(vectors, energies, strict=True)
    ]
    return stack8(weights, 0), stack8(weights, 1), energies


def sum_of(refs):
    total = refs[0][...]
    for ref in refs[1:]:
        total = total + ref[...]
    return total


def add_kernel(*refs):
    refs[-1][...] = sum_of(refs[:-1])


def add(parts):
    return pl.pallas_call(
        add_kernel,
        in_specs=[VMEM] * len(parts),
        out_specs=VMEM,
        out_shape=pltpu.VMEM(parts[0].shape, F32),
        compiler_params=pltpu.CompilerParams(vmem_limit_bytes=1024 * 1024),
        name="add",
    )(*parts)


def exchange(part, offsets):
    count = lax.axis_size("space")
    parts = [part]
    for offset in offsets:
        pairs = [(i, offset(i, count)) for i in range(count)]
        parts.append(lax.ppermute(part, "space", pairs))
    return parts


def modes_kernel(bins, *refs):
    *gram_refs, start_ref, high_ref, low_ref, modes_ref, energy_ref = refs
    rows, points = high_ref.shape
    half = rows // 2
    total = sum_of(gram_refs)
    real, imag, energies = leading(total, start_ref[...], bins)
    row, col = iota((half, 2 * rows), 0), iota((half, 2 * rows), 1)
    block, own_bin, which = row_order(col & (rows - 1))
    chosen = jnp.where(which == col // rows, block * BINS + own_bin, -1)
    spread = ones_where(row == chosen)
    wide = pick_right(jnp.concatenate([real, imag], axis=0), spread)
    to_real = wide[:8, :rows] - wide[8:, rows:]
    to_imag = wide[8:, :rows] + wide[:8, rows:]
    owner = row_order(iota((1, rows), 1))[1]
    blank = jnp.zeros((6, rows), F32)
    groups = []
    for k in range(bins):
        for m in range(MODES):
            pair = jnp.concatenate([to_real[m : m + 1], to_imag[m : m + 1]], axis=0)
            groups += [jnp.where(owner == k, pair, 0.0), blank]
    c_both = jnp.concatenate(split(jnp.concatenate(groups, axis=0)), axis=0)
    used = c_both.shape[0] // 2
    for at, size in column_chunks(points):
        both = dot(c_both, high_ref[:, at : at + size])
        out = both[:used] + (both[used:] + dot(c_both[:used], low_ref[:, at : at + size]))
        for k in range(bins):
            for m in range(MODES):
                group = (k * MODES + m) * 8
                modes_ref[k, m, :, at : at + size] = out[group : group + 2]
    stacked = jnp.concatenate(energies + [jnp.zeros((8 - MODES, half), F32)], axis=0)
    energy_ref[...] = stacked.T[:bins, :MODES]


def halves_kernel(s_ref, high_ref, low_ref):
    rows = high_ref.shape[0]
    for at, size in column_chunks(s_ref.shape[2]):
        high, low = split(s_ref[:, :, at : at + size].reshape(rows, size))
        high_ref[:, at : at + size] = high
        low_ref[:, at : at + size] = low


def halves_of(spectra):
    owners, per_owner, points = spectra.shape
    shape = (owners * per_owner, points)
    return pl.pallas_call(
        halves_kernel,
        in_specs=[VMEM],
        out_specs=[VMEM, VMEM],
        out_shape=[pltpu.VMEM(shape, BF16), pltpu.VMEM(shape, BF16)],
        compiler_params=pltpu.CompilerParams(vmem_limit_bytes=8 * 1024 * 1024),
        cost_estimate=pl.CostEstimate(flops=10**7, bytes_accessed=10**6, transcendentals=0),
        name="halves",
    )(spectra)


def modes_of(grams, start, high, low, bins):
    points = high.shape[1]
    return pl.pallas_call(
        functools.partial(modes_kernel, bins),
        in_specs=[VMEM] * (len(grams) + 3),
        out_specs=[VMEM, VMEM],
        out_shape=[
            jax.ShapeDtypeStruct((bins, MODES, 2, points), F32),
            jax.ShapeDtypeStruct((bins, MODES), F32),
        ],
        compiler_params=pltpu.CompilerParams(vmem_limit_bytes=VMEM_LIMIT),
        name="modes",
    )(*grams, start, high, low)


def on_device(snapshots, start):
    tm_count = lax.axis_size("tm")
    space_count = lax.axis_size("space")
    total_points = snapshots.shape[1] * space_count
    bins = FREQS // tm_count
    snapshots = pltpu.with_memory_space_constraint(snapshots, pltpu.HBM)
    start = pltpu.with_memory_space_constraint(start.transpose(1, 2, 3, 0), pltpu.HBM)
    sent, own = transform(snapshots, start, tm_count)
    spectra = lax.all_to_all(sent, "tm", split_axis=0, concat_axis=0, tiled=True)
    spectra = pltpu.with_memory_space_constraint(spectra, pltpu.VMEM)
    gram = partial_gram(spectra, total_points)
    near = add(exchange(gram, [lambda i, n, k=k: i ^ k for k in (1, 2, 3)]))
    grams = exchange(near, [lambda i, n, k=k: (i + 4 * k) % n for k in (1, 3, 2)])
    modes, energies = modes_of(grams, own, *halves_of(spectra), bins)
    return (modes.transpose(0, 2, 1, 3), energies)


def solution(mesh):
    in_specs = (P("tm", "space"), P())
    out_specs = (P("tm", None, None, "space"), P("tm", None))
    return jax.shard_map(
        on_device, mesh=mesh, in_specs=in_specs, out_specs=out_specs, check_vma=False
    )
```

```python
import functools
import math

import jax
import jax.numpy as jnp
import numpy as np
from jax import lax
from jax.experimental import pallas as pl
from jax.experimental.pallas import tpu as pltpu
from jax.sharding import PartitionSpec as P

NFFT = 128
FREQS = 64
NB = 32
MODES = 3
ITERS = 2
EPSILON = 1e-06
BINS = 4
BLOCKS = 2
F32 = jnp.float32
BF16 = jnp.bfloat16
CHUNK = 2048
VMEM_LIMIT = 24 * 1024 * 1024
HBM = pl.BlockSpec(memory_space=pltpu.HBM)
VMEM = pl.BlockSpec(memory_space=pltpu.VMEM)


def dft_table():
    time_ids = np.arange(NFFT)
    phase = np.arange(FREQS)[:, None] * time_ids[None, :] % NFFT
    angles = phase * (2.0 * math.pi / NFFT)
    window = 0.5 - 0.5 * np.cos(time_ids * (2.0 * math.pi / NFFT))
    scaled = window[None, :] * math.sqrt(8.0 / (3.0 * NFFT))
    table = np.stack([np.cos(angles) * scaled, -np.sin(angles) * scaled], axis=1)
    return table.reshape(2 * FREQS, NFFT).astype(np.float32)


def split(value):
    high = value.astype(BF16)
    return high, (value - high.astype(F32)).astype(BF16)


def split3(value):
    high = value.astype(BF16)
    rest = value - high.astype(F32)
    middle = rest.astype(BF16)
    return high, middle, (rest - middle.astype(F32)).astype(BF16)


def dot(left, right):
    return jnp.dot(left, right, preferred_element_type=F32)


def dot_rows(left, right):
    return lax.dot_general(left, right, (((1,), (1,)), ((), ())), preferred_element_type=F32)


def pick_right(value, select):
    rows = value.shape[0]
    parts = dot(jnp.concatenate(split3(value), axis=0), select)
    return parts[:rows] + (parts[rows : 2 * rows] + parts[2 * rows :])


def pick_left(select, value):
    high, middle, low = split3(value)
    return dot(select, high) + (dot(select, middle) + dot(select, low))


def iota(shape, dim):
    return lax.broadcasted_iota(jnp.int32, shape, dim)


def ones_where(condition):
    return jnp.where(condition, 1.0, 0.0).astype(BF16)


def row_order(row):
    pair = (row >> 3) & 1
    return (row >> 4) * BLOCKS + (((row >> 2) & 1) ^ pair), pair * 2 + ((row >> 1) & 1), row & 1


def column_chunks(points):
    size = min(CHUNK, points)
    return [(at, size) for at in range(0, points, size)]


def arrival_chunks(points):
    first = points // 4
    second = (points - first) // 2
    return [(0, first), (first, second), (first + second, points - first - second)]


def first_vectors(start, first, bins):
    lanes = NB * bins
    rows, freqs = 2 * MODES * NB, start.shape[3]
    row, col = iota((freqs, lanes), 0), iota((freqs, lanes), 1)
    picked = pick_right(start.reshape(rows, freqs), ones_where(row == first + col % bins))
    picked = jnp.where(iota((rows, lanes), 0) % NB == iota((rows, lanes), 1) // bins, picked, 0.0)
    picked = jnp.sum(picked.reshape(2 * MODES, NB, lanes), axis=1)
    vectors = [(picked[m : m + 1], picked[MODES + m : MODES + m + 1]) for m in range(MODES)]
    vectors = orthonormal(vectors, bin_ones(lanes, bins))
    return jnp.concatenate([stack8(vectors, 0), stack8(vectors, 1)], axis=0)


def transform_kernel(
    owners, table_hbm, x_hbm, start_hbm, out_ref, first_ref, table_ref, x_ref, start_ref, in_sem, small_sem
):
    times, points = x_hbm.shape
    local_blocks = times // NFFT
    chunks = arrival_chunks(points)

    def fetch(i):
        at, size = chunks[i]
        cols = pl.ds(at, size)
        return pltpu.make_async_copy(x_hbm.at[:, cols], x_ref.at[:, cols], in_sem.at[i])

    table_copy = pltpu.make_async_copy(table_hbm, table_ref, small_sem.at[0])
    start_copy = pltpu.make_async_copy(start_hbm, start_ref, small_sem.at[1])
    table_copy.start()
    start_copy.start()
    for i in range(len(chunks)):
        fetch(i).start()
    bins = FREQS // owners
    table_copy.wait()
    table = table_ref[...].reshape(owners, 2, -1, NFFT)
    table = [table, jnp.concatenate([table[:, 1:], table[:, :1]], axis=1)]
    table = [split(rows.reshape(-1, NFFT)) for rows in table]
    wide = [jnp.concatenate([high, low], axis=1) for high, low in table]
    for i, (at, size) in enumerate(chunks):
        fetch(i).wait()
        found = []
        for block in range(BLOCKS):
            x_high, x_low = split(x_ref[block * NFFT : (block + 1) * NFFT, at : at + size])
            twice = jnp.concatenate([x_high, x_high], axis=0)
            out = dot(wide[block], twice) + dot(table[block][0], x_low)
            found.append(out.reshape(owners, 8, size))
        upper = iota((owners, 8, size), 1) < 4
        out_ref[:, :8, at : at + size] = jnp.where(upper, found[0], found[1])
        out_ref[:, 8:, at : at + size] = jnp.where(upper, found[1], found[0])
        if i == 1:
            start_copy.wait()
            first = lax.axis_index("tm") * bins
            first_ref[...] = first_vectors(start_ref[...], first, bins)


def transform(snapshots, start, owners):
    times, points = snapshots.shape
    shape = (owners, 2 * FREQS // owners * (times // NFFT), points)
    count = len(arrival_chunks(points))
    table = pltpu.with_memory_space_constraint(jnp.asarray(dft_table()), pltpu.HBM)
    return pl.pallas_call(
        functools.partial(transform_kernel, owners),
        in_specs=[HBM, HBM, HBM],
        out_specs=[VMEM, VMEM],
        out_shape=[
            pltpu.VMEM(shape, F32),
            jax.ShapeDtypeStruct((16, NB * FREQS // owners), F32),
        ],
        scratch_shapes=[
            pltpu.VMEM((2 * FREQS, NFFT), F32),
            pltpu.VMEM(snapshots.shape, F32),
            pltpu.VMEM(start.shape, F32),
            pltpu.SemaphoreType.DMA((count,)),
            pltpu.SemaphoreType.DMA((2,)),
        ],
        compiler_params=pltpu.CompilerParams(vmem_limit_bytes=24 * 1024 * 1024),
        name="transform",
    )(table, snapshots, start)


def gram_kernel(scale, s_ref, out_ref):
    owners, _, points = s_ref.shape
    rows, half = owners * 8, NB * BINS
    sums = [jnp.zeros((2 * rows, rows), F32) for pair in range(2)]
    for at, size in column_chunks(points):
        for pair in range(2):
            value = s_ref[:, pair * 8 : pair * 8 + 8, at : at + size].reshape(rows, size)
            high, low = split(value)
            sums[pair] += dot_rows(jnp.concatenate([high, low], axis=0), high)
    part = jnp.zeros((2 * NB, 2 * half), F32)
    for pair in range(2):
        same, cross = sums[pair][:rows], sums[pair][rows:]
        full = (same + (cross + cross.T)) * scale
        row, col = iota((rows, rows), 0), iota((rows, rows), 1)
        full = jnp.where((row >> 1) & 1 == (col >> 1) & 1, full, 0.0)
        row, col = iota((2 * NB, rows), 0), iota((2 * NB, rows), 1)
        block, _, which = row_order((col >> 3) * 16 + pair * 8 + (col & 7))
        fold = ones_where(row == which * NB + block)
        row, col = iota((rows, 2 * half), 0), iota((rows, 2 * half), 1)
        block, own_bin, which = row_order((row >> 3) * 16 + pair * 8 + (row & 7))
        spread = ones_where(col == which * half + block * BINS + own_bin)
        part += pick_right(pick_left(fold, full), spread)
    real = part[:NB, :half] + part[NB:, half:]
    imag = part[NB:, :half] - part[:NB, half:]
    packed = jnp.where(iota(real.shape, 0) <= iota(real.shape, 1) // BINS, real, imag)
    out_ref[...] = packed


def partial_gram(spectra, total_points):
    return pl.pallas_call(
        functools.partial(gram_kernel, 1.0 / (NB * total_points)),
        in_specs=[VMEM],
        out_specs=VMEM,
        out_shape=pltpu.VMEM((NB, NB * BINS), F32),
        compiler_params=pltpu.CompilerParams(vmem_limit_bytes=VMEM_LIMIT),
        name="gram",
    )(spectra)


def bin_ones(lanes, bins):
    return ones_where(iota((lanes, lanes), 0) % bins == iota((lanes, lanes), 1) % bins)


def block_sums(terms, ones):
    blank = jnp.zeros((16 - len(terms), ones.shape[0]), F32)
    sums = pick_right(jnp.concatenate(terms + [blank], axis=0), ones)
    return [sums[i : i + 1] for i in range(len(terms))]


def overlap(e, c):
    return [e[0] * c[0] + e[1] * c[1], e[0] * c[1] - e[1] * c[0]]


def orthonormal(vectors, ones):
    left = list(vectors)
    done = []
    while left:
        head = left.pop(0)
        terms = overlap(head, head)[:1]
        for other in left:
            terms = terms + overlap(head, other)
        sums = block_sums(terms, ones)
        norm = jnp.sqrt(sums[0] + EPSILON)
        unit = (head[0] / norm, head[1] / norm)
        for i in range(len(left)):
            real, imag = sums[1 + 2 * i] / norm, sums[2 + 2 * i] / norm
            left[i] = (
                left[i][0] - (unit[0] * real - unit[1] * imag),
                left[i][1] - (unit[0] * imag + unit[1] * real),
            )
        done.append(unit)
    return done


def stack8(vectors, part):
    blank = jnp.zeros((8 - len(vectors), vectors[0][0].shape[1]), F32)
    return jnp.concatenate([v[part] for v in vectors] + [blank], axis=0)


def apply_gram(gram, vectors):
    lanes = vectors[0][0].shape[1]
    both = jnp.concatenate([stack8(vectors, 0), stack8(vectors, 1)], axis=0)
    parts = jnp.concatenate(split3(both), axis=0)
    first, second, third = dot(parts, gram[0]), dot(parts[:32], gram[1]), dot(parts[:16], gram[2])
    product = first[:16] + ((first[16:32] + second[:16]) + (first[32:] + (second[16:] + third)))
    real = product[:8, :lanes] - product[8:, lanes:]
    imag = product[8:, :lanes] + product[:8, lanes:]
    return [(real[m : m + 1], imag[m : m + 1]) for m in range(MODES)]


def leading(total, start, bins):
    lanes = start.shape[1]
    ones = bin_ones(lanes, bins)
    vectors = [(start[m : m + 1], start[8 + m : 9 + m]) for m in range(MODES)]
    row, col = iota((lanes, NB), 0), iota((lanes, NB), 1)
    packed = pick_left(ones_where(row // bins == col), total)
    row, col = iota(packed.shape, 0), iota(packed.shape, 1)
    packed = jnp.where(row % bins == col % bins, packed, 0.0)
    turned = packed.T
    row, col = row // bins, col // bins
    real = jnp.where(row <= col, packed, turned)
    imag = jnp.where(row > col, packed, jnp.where(row < col, -turned, 0.0))
    gram = split3(jnp.concatenate([real, imag], axis=1))
    for _ in range(ITERS):
        vectors = orthonormal(apply_gram(gram, vectors), ones)
    images = apply_gram(gram, vectors)
    terms = [overlap(v, g)[0] for v, g in zip(vectors, images, strict=True)]
    energies = block_sums(terms, ones)
    weights = [
        (v[0] / jnp.sqrt(NB * e), v[1] / jnp.sqrt(NB * e))
        for v, e in zip(vectors, energies, strict=True)
    ]
    return stack8(weights, 0), stack8(weights, 1), energies


def sum_of(refs):
    total = refs[0][...]
    for ref in refs[1:]:
        total = total + ref[...]
    return total


def add_kernel(*refs):
    refs[-1][...] = sum_of(refs[:-1])


def add(parts):
    return pl.pallas_call(
        add_kernel,
        in_specs=[VMEM] * len(parts),
        out_specs=VMEM,
        out_shape=pltpu.VMEM(parts[0].shape, F32),
        compiler_params=pltpu.CompilerParams(vmem_limit_bytes=1024 * 1024),
        name="add",
    )(*parts)


def exchange(part, offsets):
    count = lax.axis_size("space")
    parts = [part]
    for offset in offsets:
        pairs = [(i, offset(i, count)) for i in range(count)]
        parts.append(lax.ppermute(part, "space", pairs))
    return parts


def modes_kernel(bins, *refs):
    *gram_refs, start_ref, high_ref, low_ref, modes_ref, energy_ref = refs
    rows, points = high_ref.shape
    half = rows // 2
    total = sum_of(gram_refs)
    real, imag, energies = leading(total, start_ref[...], bins)
    row, col = iota((half, 2 * rows), 0), iota((half, 2 * rows), 1)
    block, own_bin, which = row_order(col & (rows - 1))
    chosen = jnp.where(which == col // rows, block * BINS + own_bin, -1)
    spread = ones_where(row == chosen)
    wide = pick_right(jnp.concatenate([real, imag], axis=0), spread)
    to_real = wide[:8, :rows] - wide[8:, rows:]
    to_imag = wide[8:, :rows] + wide[:8, rows:]
    owner = row_order(iota((1, rows), 1))[1]
    blank = jnp.zeros((6, rows), F32)
    groups = []
    for k in range(bins):
        for m in range(MODES):
            pair = jnp.concatenate([to_real[m : m + 1], to_imag[m : m + 1]], axis=0)
            groups += [jnp.where(owner == k, pair, 0.0), blank]
    c_both = jnp.concatenate(split(jnp.concatenate(groups, axis=0)), axis=0)
    used = c_both.shape[0] // 2
    for at, size in column_chunks(points):
        both = dot(c_both, high_ref[:, at : at + size])
        out = both[:used] + (both[used:] + dot(c_both[:used], low_ref[:, at : at + size]))
        for k in range(bins):
            for m in range(MODES):
                group = (k * MODES + m) * 8
                modes_ref[k, m, :, at : at + size] = out[group : group + 2]
    stacked = jnp.concatenate(energies + [jnp.zeros((8 - MODES, half), F32)], axis=0)
    energy_ref[...] = stacked.T[:bins, :MODES]


def halves_kernel(s_ref, high_ref, low_ref):
    rows = high_ref.shape[0]
    for at, size in column_chunks(s_ref.shape[2]):
        high, low = split(s_ref[:, :, at : at + size].reshape(rows, size))
        high_ref[:, at : at + size] = high
        low_ref[:, at : at + size] = low


def halves_of(spectra):
    owners, per_owner, points = spectra.shape
    shape = (owners * per_owner, points)
    return pl.pallas_call(
        halves_kernel,
        in_specs=[VMEM],
        out_specs=[VMEM, VMEM],
        out_shape=[pltpu.VMEM(shape, BF16), pltpu.VMEM(shape, BF16)],
        compiler_params=pltpu.CompilerParams(vmem_limit_bytes=8 * 1024 * 1024),
        cost_estimate=pl.CostEstimate(flops=10**7, bytes_accessed=10**6, transcendentals=0),
        name="halves",
    )(spectra)


def modes_of(grams, start, high, low, bins):
    points = high.shape[1]
    return pl.pallas_call(
        functools.partial(modes_kernel, bins),
        in_specs=[VMEM] * (len(grams) + 3),
        out_specs=[VMEM, VMEM],
        out_shape=[
            jax.ShapeDtypeStruct((bins, MODES, 2, points), F32),
            jax.ShapeDtypeStruct((bins, MODES), F32),
        ],
        compiler_params=pltpu.CompilerParams(vmem_limit_bytes=VMEM_LIMIT),
        name="modes",
    )(*grams, start, high, low)


def on_device(snapshots, start):
    tm_count = lax.axis_size("tm")
    space_count = lax.axis_size("space")
    total_points = snapshots.shape[1] * space_count
    bins = FREQS // tm_count
    snapshots = pltpu.with_memory_space_constraint(snapshots, pltpu.HBM)
    start = pltpu.with_memory_space_constraint(start.transpose(1, 2, 3, 0), pltpu.HBM)
    sent, own = transform(snapshots, start, tm_count)
    spectra = lax.all_to_all(sent, "tm", split_axis=0, concat_axis=0, tiled=True)
    spectra = pltpu.with_memory_space_constraint(spectra, pltpu.VMEM)
    gram = partial_gram(spectra, total_points)
    near = add(exchange(gram, [lambda i, n, k=k: i ^ k for k in (1, 2, 3)]))
    grams = exchange(near, [lambda i, n, k=k: (i + 4 * k) % n for k in (1, 3, 2)])
    modes, energies = modes_of(grams, own, *halves_of(spectra), bins)
    return (modes.transpose(0, 2, 1, 3), energies)


def solution(mesh):
    in_specs = (P("tm", "space"), P())
    out_specs = (P("tm", None, None, "space"), P("tm", None))
    return jax.shard_map(
        on_device, mesh=mesh, in_specs=in_specs, out_specs=out_specs, check_vma=False
    )
```

```python
import functools
import math

import jax
import jax.numpy as jnp
import numpy as np
from jax import lax
from jax.experimental import pallas as pl
from jax.experimental.pallas import tpu as pltpu
from jax.sharding import PartitionSpec as P

NFFT = 128
FREQS = 64
NB = 32
MODES = 3
ITERS = 2
EPSILON = 1e-06
BINS = 4
BLOCKS = 2
F32 = jnp.float32
BF16 = jnp.bfloat16
CHUNK = 2048
VMEM_LIMIT = 24 * 1024 * 1024
HBM = pl.BlockSpec(memory_space=pltpu.HBM)
VMEM = pl.BlockSpec(memory_space=pltpu.VMEM)


def dft_table():
    time_ids = np.arange(NFFT)
    phase = np.arange(FREQS)[:, None] * time_ids[None, :] % NFFT
    angles = phase * (2.0 * math.pi / NFFT)
    window = 0.5 - 0.5 * np.cos(time_ids * (2.0 * math.pi / NFFT))
    scaled = window[None, :] * math.sqrt(8.0 / (3.0 * NFFT))
    table = np.stack([np.cos(angles) * scaled, -np.sin(angles) * scaled], axis=1)
    return table.reshape(2 * FREQS, NFFT).astype(np.float32)


def split(value):
    high = value.astype(BF16)
    return high, (value - high.astype(F32)).astype(BF16)


def split3(value):
    high = value.astype(BF16)
    rest = value - high.astype(F32)
    middle = rest.astype(BF16)
    return high, middle, (rest - middle.astype(F32)).astype(BF16)


def dot(left, right):
    return jnp.dot(left, right, preferred_element_type=F32)


def dot_rows(left, right):
    return lax.dot_general(left, right, (((1,), (1,)), ((), ())), preferred_element_type=F32)


def pick_right(value, select):
    rows = value.shape[0]
    parts = dot(jnp.concatenate(split3(value), axis=0), select)
    return parts[:rows] + (parts[rows : 2 * rows] + parts[2 * rows :])


def pick_left(select, value):
    high, middle, low = split3(value)
    return dot(select, high) + (dot(select, middle) + dot(select, low))


def iota(shape, dim):
    return lax.broadcasted_iota(jnp.int32, shape, dim)


def ones_where(condition):
    return jnp.where(condition, 1.0, 0.0).astype(BF16)


def row_order(row):
    return row >> 3, (row >> 1) & 3, row & 1


def column_chunks(points):
    size = min(CHUNK, points)
    return [(at, size) for at in range(0, points, size)]


def arrival_chunks(points):
    first = points // 4
    second = (points - first) // 2
    return [(0, first), (first, second), (first + second, points - first - second)]


def first_vectors(start, first, bins):
    lanes = NB * bins
    rows, freqs = 2 * MODES * NB, start.shape[3]
    row, col = iota((freqs, lanes), 0), iota((freqs, lanes), 1)
    picked = pick_right(start.reshape(rows, freqs), ones_where(row == first + col % bins))
    picked = jnp.where(iota((rows, lanes), 0) % NB == iota((rows, lanes), 1) // bins, picked, 0.0)
    picked = jnp.sum(picked.reshape(2 * MODES, NB, lanes), axis=1)
    vectors = [(picked[m : m + 1], picked[MODES + m : MODES + m + 1]) for m in range(MODES)]
    vectors = orthonormal(vectors, bin_ones(lanes, bins))
    return jnp.concatenate([stack8(vectors, 0), stack8(vectors, 1)], axis=0)


def transform_kernel(
    owners, table_hbm, x_hbm, start_hbm, out_ref, first_ref, table_ref, x_ref, start_ref, in_sem, small_sem
):
    times, points = x_hbm.shape
    local_blocks = times // NFFT
    chunks = arrival_chunks(points)

    def fetch(i):
        at, size = chunks[i]
        cols = pl.ds(at, size)
        return pltpu.make_async_copy(x_hbm.at[:, cols], x_ref.at[:, cols], in_sem.at[i])

    table_copy = pltpu.make_async_copy(table_hbm, table_ref, small_sem.at[0])
    start_copy = pltpu.make_async_copy(start_hbm, start_ref, small_sem.at[1])
    table_copy.start()
    start_copy.start()
    for i in range(len(chunks)):
        fetch(i).start()
    bins = FREQS // owners
    table_copy.wait()
    high, middle, low = split3(table_ref[...])
    wide = jnp.concatenate([high, middle, low, high, middle, high], axis=1)
    for i, (at, size) in enumerate(chunks):
        fetch(i).wait()
        x = x_ref[:, at : at + size]
        x_high, x_middle, x_low = split3(jnp.concatenate([x[:NFFT], x[NFFT:]], axis=1))
        out = dot(wide, jnp.concatenate([x_high, x_high, x_high, x_middle, x_middle, x_low], axis=0))
        for block in range(BLOCKS):
            rows, cols = slice(block * 8, block * 8 + 8), slice(block * size, block * size + size)
            out_ref[:, rows, at : at + size] = out[:, cols].reshape(owners, 8, size)
        if i == 1:
            start_copy.wait()
            first = lax.axis_index("tm") * bins
            first_ref[...] = first_vectors(start_ref[...], first, bins)


def transform(snapshots, start, owners):
    times, points = snapshots.shape
    shape = (owners, 2 * FREQS // owners * (times // NFFT), points)
    count = len(arrival_chunks(points))
    table = pltpu.with_memory_space_constraint(jnp.asarray(dft_table()), pltpu.HBM)
    return pl.pallas_call(
        functools.partial(transform_kernel, owners),
        in_specs=[HBM, HBM, HBM],
        out_specs=[VMEM, VMEM],
        out_shape=[
            pltpu.VMEM(shape, F32),
            jax.ShapeDtypeStruct((16, NB * FREQS // owners), F32),
        ],
        scratch_shapes=[
            pltpu.VMEM((2 * FREQS, NFFT), F32),
            pltpu.VMEM(snapshots.shape, F32),
            pltpu.VMEM(start.shape, F32),
            pltpu.SemaphoreType.DMA((count,)),
            pltpu.SemaphoreType.DMA((2,)),
        ],
        compiler_params=pltpu.CompilerParams(vmem_limit_bytes=24 * 1024 * 1024),
        name="transform",
    )(table, snapshots, start)


def gram_kernel(scale, s_ref, out_ref):
    points = s_ref.shape[2]
    rows, half = 2 * NB * BINS, NB * BINS
    sums = jnp.zeros((2 * rows, rows), F32)
    for at, size in column_chunks(points):
        high, low = split(s_ref[:, :, at : at + size].reshape(rows, size))
        sums += dot_rows(jnp.concatenate([high, low], axis=0), high)
    cross = sums[rows:]
    full = (sums[:rows] + (cross + cross.T)) * scale
    row, col = iota((rows, rows), 0), iota((rows, rows), 1)
    full = jnp.where(row_order(row)[1] == row_order(col)[1], full, 0.0)
    row, col = iota((2 * NB, rows), 0), iota((2 * NB, rows), 1)
    block, _, which = row_order(col)
    fold = ones_where(row == which * NB + block)
    row, col = iota((rows, 2 * half), 0), iota((rows, 2 * half), 1)
    block, own_bin, which = row_order(row)
    spread = ones_where(col == which * half + block * BINS + own_bin)
    part = pick_right(pick_left(fold, full), spread)
    real = part[:NB, :half] + part[NB:, half:]
    imag = part[NB:, :half] - part[:NB, half:]
    packed = jnp.where(iota(real.shape, 0) <= iota(real.shape, 1) // BINS, real, imag)
    out_ref[...] = packed


def partial_gram(spectra, total_points):
    return pl.pallas_call(
        functools.partial(gram_kernel, 1.0 / (NB * total_points)),
        in_specs=[VMEM],
        out_specs=VMEM,
        out_shape=pltpu.VMEM((NB, NB * BINS), F32),
        compiler_params=pltpu.CompilerParams(vmem_limit_bytes=VMEM_LIMIT),
        name="gram",
    )(spectra)


def bin_ones(lanes, bins):
    return ones_where(iota((lanes, lanes), 0) % bins == iota((lanes, lanes), 1) % bins)


def block_sums(terms, ones):
    blank = jnp.zeros((16 - len(terms), ones.shape[0]), F32)
    sums = pick_right(jnp.concatenate(terms + [blank], axis=0), ones)
    return [sums[i : i + 1] for i in range(len(terms))]


def overlap(e, c):
    return [e[0] * c[0] + e[1] * c[1], e[0] * c[1] - e[1] * c[0]]


def orthonormal(vectors, ones):
    left = list(vectors)
    done = []
    while left:
        head = left.pop(0)
        terms = overlap(head, head)[:1]
        for other in left:
            terms = terms + overlap(head, other)
        sums = block_sums(terms, ones)
        norm = jnp.sqrt(sums[0] + EPSILON)
        unit = (head[0] / norm, head[1] / norm)
        for i in range(len(left)):
            real, imag = sums[1 + 2 * i] / norm, sums[2 + 2 * i] / norm
            left[i] = (
                left[i][0] - (unit[0] * real - unit[1] * imag),
                left[i][1] - (unit[0] * imag + unit[1] * real),
            )
        done.append(unit)
    return done


def stack8(vectors, part):
    blank = jnp.zeros((8 - len(vectors), vectors[0][0].shape[1]), F32)
    return jnp.concatenate([v[part] for v in vectors] + [blank], axis=0)


def apply_gram(gram, vectors):
    lanes = vectors[0][0].shape[1]
    both = jnp.concatenate([stack8(vectors, 0), stack8(vectors, 1)], axis=0)
    parts = jnp.concatenate(split3(both), axis=0)
    first, second, third = dot(parts, gram[0]), dot(parts[:32], gram[1]), dot(parts[:16], gram[2])
    product = first[:16] + ((first[16:32] + second[:16]) + (first[32:] + (second[16:] + third)))
    real = product[:8, :lanes] - product[8:, lanes:]
    imag = product[8:, :lanes] + product[:8, lanes:]
    return [(real[m : m + 1], imag[m : m + 1]) for m in range(MODES)]


def leading(total, start, bins):
    lanes = start.shape[1]
    ones = bin_ones(lanes, bins)
    vectors = [(start[m : m + 1], start[8 + m : 9 + m]) for m in range(MODES)]
    row, col = iota((lanes, NB), 0), iota((lanes, NB), 1)
    packed = pick_left(ones_where(row // bins == col), total)
    row, col = iota(packed.shape, 0), iota(packed.shape, 1)
    packed = jnp.where(row % bins == col % bins, packed, 0.0)
    turned = packed.T
    row, col = row // bins, col // bins
    real = jnp.where(row <= col, packed, turned)
    imag = jnp.where(row > col, packed, jnp.where(row < col, -turned, 0.0))
    gram = split3(jnp.concatenate([real, imag], axis=1))
    for _ in range(ITERS):
        vectors = orthonormal(apply_gram(gram, vectors), ones)
    images = apply_gram(gram, vectors)
    terms = [overlap(v, g)[0] for v, g in zip(vectors, images, strict=True)]
    energies = block_sums(terms, ones)
    weights = [
        (v[0] / jnp.sqrt(NB * e), v[1] / jnp.sqrt(NB * e))
        for v, e in zip(vectors, energies, strict=True)
    ]
    return stack8(weights, 0), stack8(weights, 1), energies


def sum_of(refs):
    total = refs[0][...]
    for ref in refs[1:]:
        total = total + ref[...]
    return total


def add_kernel(*refs):
    refs[-1][...] = sum_of(refs[:-1])


def add(parts):
    return pl.pallas_call(
        add_kernel,
        in_specs=[VMEM] * len(parts),
        out_specs=VMEM,
        out_shape=pltpu.VMEM(parts[0].shape, F32),
        compiler_params=pltpu.CompilerParams(vmem_limit_bytes=1024 * 1024),
        name="add",
    )(*parts)


def exchange(part, offsets):
    count = lax.axis_size("space")
    parts = [part]
    for offset in offsets:
        pairs = [(i, offset(i, count)) for i in range(count)]
        parts.append(lax.ppermute(part, "space", pairs))
    return parts


def modes_kernel(bins, *refs):
    *gram_refs, start_ref, high_ref, low_ref, modes_ref, energy_ref = refs
    rows, points = high_ref.shape
    half = rows // 2
    total = sum_of(gram_refs)
    real, imag, energies = leading(total, start_ref[...], bins)
    row, col = iota((half, 2 * rows), 0), iota((half, 2 * rows), 1)
    block, own_bin, which = row_order(col & (rows - 1))
    chosen = jnp.where(which == col // rows, block * BINS + own_bin, -1)
    spread = ones_where(row == chosen)
    wide = pick_right(jnp.concatenate([real, imag], axis=0), spread)
    to_real = wide[:8, :rows] - wide[8:, rows:]
    to_imag = wide[8:, :rows] + wide[:8, rows:]
    owner = row_order(iota((1, rows), 1))[1]
    blank = jnp.zeros((6, rows), F32)
    groups = []
    for k in range(bins):
        for m in range(MODES):
            pair = jnp.concatenate([to_real[m : m + 1], to_imag[m : m + 1]], axis=0)
            groups += [jnp.where(owner == k, pair, 0.0), blank]
    c_both = jnp.concatenate(split(jnp.concatenate(groups, axis=0)), axis=0)
    used = c_both.shape[0] // 2
    for at, size in column_chunks(points):
        both = dot(c_both, high_ref[:, at : at + size])
        out = both[:used] + (both[used:] + dot(c_both[:used], low_ref[:, at : at + size]))
        for k in range(bins):
            for m in range(MODES):
                group = (k * MODES + m) * 8
                modes_ref[k, m, :, at : at + size] = out[group : group + 2]
    stacked = jnp.concatenate(energies + [jnp.zeros((8 - MODES, half), F32)], axis=0)
    energy_ref[...] = stacked.T[:bins, :MODES]


def halves_kernel(s_ref, high_ref, low_ref):
    rows = high_ref.shape[0]
    for at, size in column_chunks(s_ref.shape[2]):
        high, low = split(s_ref[:, :, at : at + size].reshape(rows, size))
        high_ref[:, at : at + size] = high
        low_ref[:, at : at + size] = low


def halves_of(spectra):
    owners, per_owner, points = spectra.shape
    shape = (owners * per_owner, points)
    return pl.pallas_call(
        halves_kernel,
        in_specs=[VMEM],
        out_specs=[VMEM, VMEM],
        out_shape=[pltpu.VMEM(shape, BF16), pltpu.VMEM(shape, BF16)],
        compiler_params=pltpu.CompilerParams(vmem_limit_bytes=8 * 1024 * 1024),
        cost_estimate=pl.CostEstimate(flops=10**7, bytes_accessed=10**6, transcendentals=0),
        name="halves",
    )(spectra)


def modes_of(grams, start, high, low, bins):
    points = high.shape[1]
    return pl.pallas_call(
        functools.partial(modes_kernel, bins),
        in_specs=[VMEM] * (len(grams) + 3),
        out_specs=[VMEM, VMEM],
        out_shape=[
            jax.ShapeDtypeStruct((bins, MODES, 2, points), F32),
            jax.ShapeDtypeStruct((bins, MODES), F32),
        ],
        compiler_params=pltpu.CompilerParams(vmem_limit_bytes=VMEM_LIMIT),
        name="modes",
    )(*grams, start, high, low)


def on_device(snapshots, start):
    tm_count = lax.axis_size("tm")
    space_count = lax.axis_size("space")
    total_points = snapshots.shape[1] * space_count
    bins = FREQS // tm_count
    snapshots = pltpu.with_memory_space_constraint(snapshots, pltpu.HBM)
    start = pltpu.with_memory_space_constraint(start.transpose(1, 2, 3, 0), pltpu.HBM)
    sent, own = transform(snapshots, start, tm_count)
    spectra = lax.all_to_all(sent, "tm", split_axis=0, concat_axis=0, tiled=True)
    spectra = pltpu.with_memory_space_constraint(spectra, pltpu.VMEM)
    gram = partial_gram(spectra, total_points)
    near = add(exchange(gram, [lambda i, n, k=k: i ^ k for k in (1, 2, 3)]))
    grams = exchange(near, [lambda i, n, k=k: (i + 4 * k) % n for k in (1, 3, 2)])
    modes, energies = modes_of(grams, own, *halves_of(spectra), bins)
    return (modes.transpose(0, 2, 1, 3), energies)


def solution(mesh):
    in_specs = (P("tm", "space"), P())
    out_specs = (P("tm", None, None, "space"), P("tm", None))
    return jax.shard_map(
        on_device, mesh=mesh, in_specs=in_specs, out_specs=out_specs, check_vma=False
    )
```

```python
import functools
import math

import jax
import jax.numpy as jnp
import numpy as np
from jax import lax
from jax.experimental import pallas as pl
from jax.experimental.pallas import tpu as pltpu
from jax.sharding import PartitionSpec as P

NFFT = 128
FREQS = 64
NB = 32
MODES = 3
ITERS = 2
EPSILON = 1e-06
BINS = 4
BLOCKS = 2
F32 = jnp.float32
BF16 = jnp.bfloat16
CHUNK = 2048
VMEM_LIMIT = 24 * 1024 * 1024
HBM = pl.BlockSpec(memory_space=pltpu.HBM)
VMEM = pl.BlockSpec(memory_space=pltpu.VMEM)


def dft_table():
    time_ids = np.arange(NFFT)
    phase = np.arange(FREQS)[:, None] * time_ids[None, :] % NFFT
    angles = phase * (2.0 * math.pi / NFFT)
    window = 0.5 - 0.5 * np.cos(time_ids * (2.0 * math.pi / NFFT))
    scaled = window[None, :] * math.sqrt(8.0 / (3.0 * NFFT))
    table = np.stack([np.cos(angles) * scaled, -np.sin(angles) * scaled], axis=1)
    return table.reshape(2 * FREQS, NFFT).astype(np.float32)


def split(value):
    high = value.astype(BF16)
    return high, (value - high.astype(F32)).astype(BF16)


def split3(value):
    high = value.astype(BF16)
    rest = value - high.astype(F32)
    middle = rest.astype(BF16)
    return high, middle, (rest - middle.astype(F32)).astype(BF16)


def dot(left, right):
    return jnp.dot(left, right, preferred_element_type=F32)


def dot_rows(left, right):
    return lax.dot_general(left, right, (((1,), (1,)), ((), ())), preferred_element_type=F32)


def pick_right(value, select):
    rows = value.shape[0]
    parts = dot(jnp.concatenate(split3(value), axis=0), select)
    return parts[:rows] + (parts[rows : 2 * rows] + parts[2 * rows :])


def pick_left(select, value):
    high, middle, low = split3(value)
    return dot(select, high) + (dot(select, middle) + dot(select, low))


def iota(shape, dim):
    return lax.broadcasted_iota(jnp.int32, shape, dim)


def ones_where(condition):
    return jnp.where(condition, 1.0, 0.0).astype(BF16)


def row_order(row):
    return row >> 3, (row >> 1) & 3, row & 1


def column_chunks(points):
    size = min(CHUNK, points)
    return [(at, size) for at in range(0, points, size)]


def arrival_chunks(points):
    first = points // 4
    second = (points - first) // 2
    return [(0, first), (first, second), (first + second, points - first - second)]


def first_vectors(start, first, bins):
    lanes = NB * bins
    rows, freqs = 2 * MODES * NB, start.shape[3]
    row, col = iota((freqs, lanes), 0), iota((freqs, lanes), 1)
    picked = pick_right(start.reshape(rows, freqs), ones_where(row == first + col % bins))
    picked = jnp.where(iota((rows, lanes), 0) % NB == iota((rows, lanes), 1) // bins, picked, 0.0)
    picked = jnp.sum(picked.reshape(2 * MODES, NB, lanes), axis=1)
    vectors = [(picked[m : m + 1], picked[MODES + m : MODES + m + 1]) for m in range(MODES)]
    vectors = orthonormal(vectors, bin_ones(lanes, bins))
    return jnp.concatenate([stack8(vectors, 0), stack8(vectors, 1)], axis=0)


def transform_kernel(
    owners, table_hbm, x_hbm, start_hbm, out_ref, start_ref, table_ref, x_ref, in_sem, small_sem
):
    times, points = x_hbm.shape
    local_blocks = times // NFFT
    chunks = arrival_chunks(points)

    def fetch(i):
        at, size = chunks[i]
        cols = pl.ds(at, size)
        return pltpu.make_async_copy(x_hbm.at[:, cols], x_ref.at[:, cols], in_sem.at[i])

    table_copy = pltpu.make_async_copy(table_hbm, table_ref, small_sem.at[0])
    start_copy = pltpu.make_async_copy(start_hbm, start_ref, small_sem.at[1])
    table_copy.start()
    start_copy.start()
    for i in range(len(chunks)):
        fetch(i).start()
    table_copy.wait()
    high, middle, low = split3(table_ref[...])
    wide = jnp.concatenate([high, middle, low, high, middle, high], axis=1)
    for i, (at, size) in enumerate(chunks):
        fetch(i).wait()
        x = x_ref[:, at : at + size]
        x_high, x_middle, x_low = split3(jnp.concatenate([x[:NFFT], x[NFFT:]], axis=1))
        out = dot(wide, jnp.concatenate([x_high, x_high, x_high, x_middle, x_middle, x_low], axis=0))
        for block in range(BLOCKS):
            rows, cols = slice(block * 8, block * 8 + 8), slice(block * size, block * size + size)
            out_ref[:, rows, at : at + size] = out[:, cols].reshape(owners, 8, size)
    start_copy.wait()


def transform(snapshots, start, owners):
    times, points = snapshots.shape
    shape = (owners, 2 * FREQS // owners * (times // NFFT), points)
    count = len(arrival_chunks(points))
    table = pltpu.with_memory_space_constraint(jnp.asarray(dft_table()), pltpu.HBM)
    return pl.pallas_call(
        functools.partial(transform_kernel, owners),
        in_specs=[HBM, HBM, HBM],
        out_specs=[VMEM, VMEM],
        out_shape=[
            pltpu.VMEM(shape, F32),
            pltpu.VMEM(start.shape, F32),
        ],
        scratch_shapes=[
            pltpu.VMEM((2 * FREQS, NFFT), F32),
            pltpu.VMEM(snapshots.shape, F32),
            pltpu.SemaphoreType.DMA((count,)),
            pltpu.SemaphoreType.DMA((2,)),
        ],
        compiler_params=pltpu.CompilerParams(vmem_limit_bytes=24 * 1024 * 1024),
        name="transform",
    )(table, snapshots, start)


def gram_kernel(scale, s_ref, start_ref, out_ref, first_ref):
    points = s_ref.shape[2]
    rows, half = 2 * NB * BINS, NB * BINS
    sums = jnp.zeros((2 * rows, rows), F32)
    for at, size in column_chunks(points):
        high, low = split(s_ref[:, :, at : at + size].reshape(rows, size))
        sums += dot_rows(jnp.concatenate([high, low], axis=0), high)
        if at == 0:
            first = lax.axis_index("tm") * BINS
            first_ref[...] = first_vectors(start_ref[...], first, BINS)
    cross = sums[rows:]
    full = (sums[:rows] + (cross + cross.T)) * scale
    row, col = iota((rows, rows), 0), iota((rows, rows), 1)
    full = jnp.where(row_order(row)[1] == row_order(col)[1], full, 0.0)
    row, col = iota((2 * NB, rows), 0), iota((2 * NB, rows), 1)
    block, _, which = row_order(col)
    fold = ones_where(row == which * NB + block)
    row, col = iota((rows, 2 * half), 0), iota((rows, 2 * half), 1)
    block, own_bin, which = row_order(row)
    spread = ones_where(col == which * half + block * BINS + own_bin)
    part = pick_right(pick_left(fold, full), spread)
    real = part[:NB, :half] + part[NB:, half:]
    imag = part[NB:, :half] - part[:NB, half:]
    packed = jnp.where(iota(real.shape, 0) <= iota(real.shape, 1) // BINS, real, imag)
    out_ref[...] = packed


def partial_gram(spectra, start, total_points):
    return pl.pallas_call(
        functools.partial(gram_kernel, 1.0 / (NB * total_points)),
        in_specs=[VMEM, VMEM],
        out_specs=[VMEM, VMEM],
        out_shape=[pltpu.VMEM((NB, NB * BINS), F32), pltpu.VMEM((16, NB * BINS), F32)],
        compiler_params=pltpu.CompilerParams(vmem_limit_bytes=VMEM_LIMIT),
        name="gram",
    )(spectra, start)


def bin_ones(lanes, bins):
    return ones_where(iota((lanes, lanes), 0) % bins == iota((lanes, lanes), 1) % bins)


def block_sums(terms, ones):
    blank = jnp.zeros((16 - len(terms), ones.shape[0]), F32)
    sums = pick_right(jnp.concatenate(terms + [blank], axis=0), ones)
    return [sums[i : i + 1] for i in range(len(terms))]


def overlap(e, c):
    return [e[0] * c[0] + e[1] * c[1], e[0] * c[1] - e[1] * c[0]]


def orthonormal(vectors, ones):
    left = list(vectors)
    done = []
    while left:
        head = left.pop(0)
        terms = overlap(head, head)[:1]
        for other in left:
            terms = terms + overlap(head, other)
        sums = block_sums(terms, ones)
        norm = jnp.sqrt(sums[0] + EPSILON)
        unit = (head[0] / norm, head[1] / norm)
        for i in range(len(left)):
            real, imag = sums[1 + 2 * i] / norm, sums[2 + 2 * i] / norm
            left[i] = (
                left[i][0] - (unit[0] * real - unit[1] * imag),
                left[i][1] - (unit[0] * imag + unit[1] * real),
            )
        done.append(unit)
    return done


def stack8(vectors, part):
    blank = jnp.zeros((8 - len(vectors), vectors[0][0].shape[1]), F32)
    return jnp.concatenate([v[part] for v in vectors] + [blank], axis=0)


def apply_gram(gram, vectors):
    lanes = vectors[0][0].shape[1]
    both = jnp.concatenate([stack8(vectors, 0), stack8(vectors, 1)], axis=0)
    parts = jnp.concatenate(split3(both), axis=0)
    first, second, third = dot(parts, gram[0]), dot(parts[:32], gram[1]), dot(parts[:16], gram[2])
    product = first[:16] + ((first[16:32] + second[:16]) + (first[32:] + (second[16:] + third)))
    real = product[:8, :lanes] - product[8:, lanes:]
    imag = product[8:, :lanes] + product[:8, lanes:]
    return [(real[m : m + 1], imag[m : m + 1]) for m in range(MODES)]


def leading(total, start, bins):
    lanes = start.shape[1]
    ones = bin_ones(lanes, bins)
    vectors = [(start[m : m + 1], start[8 + m : 9 + m]) for m in range(MODES)]
    row, col = iota((lanes, NB), 0), iota((lanes, NB), 1)
    packed = pick_left(ones_where(row // bins == col), total)
    row, col = iota(packed.shape, 0), iota(packed.shape, 1)
    packed = jnp.where(row % bins == col % bins, packed, 0.0)
    turned = packed.T
    row, col = row // bins, col // bins
    real = jnp.where(row <= col, packed, turned)
    imag = jnp.where(row > col, packed, jnp.where(row < col, -turned, 0.0))
    gram = split3(jnp.concatenate([real, imag], axis=1))
    for _ in range(ITERS):
        vectors = orthonormal(apply_gram(gram, vectors), ones)
    images = apply_gram(gram, vectors)
    terms = [overlap(v, g)[0] for v, g in zip(vectors, images, strict=True)]
    energies = block_sums(terms, ones)
    weights = [
        (v[0] / jnp.sqrt(NB * e), v[1] / jnp.sqrt(NB * e))
        for v, e in zip(vectors, energies, strict=True)
    ]
    return stack8(weights, 0), stack8(weights, 1), energies


def sum_of(refs):
    total = refs[0][...]
    for ref in refs[1:]:
        total = total + ref[...]
    return total


def add_kernel(*refs):
    refs[-1][...] = sum_of(refs[:-1])


def add(parts):
    return pl.pallas_call(
        add_kernel,
        in_specs=[VMEM] * len(parts),
        out_specs=VMEM,
        out_shape=pltpu.VMEM(parts[0].shape, F32),
        compiler_params=pltpu.CompilerParams(vmem_limit_bytes=1024 * 1024),
        name="add",
    )(*parts)


def exchange(part, offsets):
    count = lax.axis_size("space")
    parts = [part]
    for offset in offsets:
        pairs = [(i, offset(i, count)) for i in range(count)]
        parts.append(lax.ppermute(part, "space", pairs))
    return parts


def modes_kernel(bins, *refs):
    *gram_refs, start_ref, high_ref, low_ref, modes_ref, energy_ref = refs
    rows, points = high_ref.shape
    half = rows // 2
    total = sum_of(gram_refs)
    real, imag, energies = leading(total, start_ref[...], bins)
    row, col = iota((half, 2 * rows), 0), iota((half, 2 * rows), 1)
    block, own_bin, which = row_order(col & (rows - 1))
    chosen = jnp.where(which == col // rows, block * BINS + own_bin, -1)
    spread = ones_where(row == chosen)
    wide = pick_right(jnp.concatenate([real, imag], axis=0), spread)
    to_real = wide[:8, :rows] - wide[8:, rows:]
    to_imag = wide[8:, :rows] + wide[:8, rows:]
    owner = row_order(iota((1, rows), 1))[1]
    blank = jnp.zeros((6, rows), F32)
    groups = []
    for k in range(bins):
        for m in range(MODES):
            pair = jnp.concatenate([to_real[m : m + 1], to_imag[m : m + 1]], axis=0)
            groups += [jnp.where(owner == k, pair, 0.0), blank]
    c_both = jnp.concatenate(split(jnp.concatenate(groups, axis=0)), axis=0)
    used = c_both.shape[0] // 2
    for at, size in column_chunks(points):
        both = dot(c_both, high_ref[:, at : at + size])
        out = both[:used] + (both[used:] + dot(c_both[:used], low_ref[:, at : at + size]))
        for k in range(bins):
            for m in range(MODES):
                group = (k * MODES + m) * 8
                modes_ref[k, m, :, at : at + size] = out[group : group + 2]
    stacked = jnp.concatenate(energies + [jnp.zeros((8 - MODES, half), F32)], axis=0)
    energy_ref[...] = stacked.T[:bins, :MODES]


def halves_kernel(s_ref, high_ref, low_ref):
    rows = high_ref.shape[0]
    for at, size in column_chunks(s_ref.shape[2]):
        high, low = split(s_ref[:, :, at : at + size].reshape(rows, size))
        high_ref[:, at : at + size] = high
        low_ref[:, at : at + size] = low


def halves_of(spectra):
    owners, per_owner, points = spectra.shape
    shape = (owners * per_owner, points)
    return pl.pallas_call(
        halves_kernel,
        in_specs=[VMEM],
        out_specs=[VMEM, VMEM],
        out_shape=[
            pltpu.VMEM(shape, BF16),
            pltpu.VMEM(shape, BF16),
        ],
        compiler_params=pltpu.CompilerParams(vmem_limit_bytes=8 * 1024 * 1024),
        cost_estimate=pl.CostEstimate(flops=10**7, bytes_accessed=10**6, transcendentals=0),
        name="halves",
    )(spectra)


def modes_of(grams, start, high, low, bins):
    points = high.shape[1]
    return pl.pallas_call(
        functools.partial(modes_kernel, bins),
        in_specs=[VMEM] * (len(grams) + 3),
        out_specs=[VMEM, VMEM],
        out_shape=[
            jax.ShapeDtypeStruct((bins, MODES, 2, points), F32),
            jax.ShapeDtypeStruct((bins, MODES), F32),
        ],
        compiler_params=pltpu.CompilerParams(vmem_limit_bytes=VMEM_LIMIT),
        name="modes",
    )(*grams, start, high, low)


def on_device(snapshots, start):
    tm_count = lax.axis_size("tm")
    space_count = lax.axis_size("space")
    total_points = snapshots.shape[1] * space_count
    bins = FREQS // tm_count
    snapshots = pltpu.with_memory_space_constraint(snapshots, pltpu.HBM)
    start = pltpu.with_memory_space_constraint(start.transpose(1, 2, 3, 0), pltpu.HBM)
    sent, kept = transform(snapshots, start, tm_count)
    spectra = lax.all_to_all(sent, "tm", split_axis=0, concat_axis=0, tiled=True)
    spectra = pltpu.with_memory_space_constraint(spectra, pltpu.VMEM)
    gram, own = partial_gram(spectra, kept, total_points)
    near = add(exchange(gram, [lambda i, n, k=k: i ^ k for k in (1, 2, 3)]))
    grams = exchange(near, [lambda i, n, k=k: (i + 4 * k) % n for k in (1, 3, 2)])
    modes, energies = modes_of(grams, own, *halves_of(spectra), bins)
    return (modes.transpose(0, 2, 1, 3), energies)


def solution(mesh):
    in_specs = (P("tm", "space"), P())
    out_specs = (P("tm", None, None, "space"), P("tm", None))
    return jax.shard_map(
        on_device, mesh=mesh, in_specs=in_specs, out_specs=out_specs, check_vma=False
    )
```
